32 devices in a mesh: group: 2 (over x), dp: 16 (over z, y, core).
Axes of the slice: x: 2, y: 2, z: 4, core: 2. Of those that a mesh axis runs over, the one named last changes fastest.
Arguments:
- tokens: bfloat16 [4096, 8192], P(('group', 'dp')), parts along dimension 0, may hold values from -6 to 6
- frozen_projection_weight: bfloat16 [8192, 1024], replicated, may hold values from -0.0625 to 0.0625
- adapter_down: bfloat16 [256, 8192, 128], P('group', 'dp'), parts along dimension 0, may hold values from -0.0625 to 0.0625
- adapter_up: bfloat16 [256, 128, 1024], P('group', 'dp'), parts along dimension 0, may hold values from -0.5 to 0.5
- adapter_rank: int32 [256], P('group'), parts along dimension 0, may hold values from 8 to 128, as said below
- request_adapter: int32 [32, 3], P('group'), parts along dimension 0, may hold values from 0 to 127
- request_length: int32 [32, 3], P('group'), parts along dimension 0, may hold values from 1 to 64, 128 in all within a row
Outputs:
- projected: bfloat16 [4096, 1024], P(('group', 'dp')), parts along dimension 0
The draws below stay inside these ranges and needn't reach their ends.
There are 2 independent parts, one for each index of `group`. The reference program is written for one: setup_inputs(seed, part) draws one part's arguments, and reference() takes and returns one part's arrays. A program takes and returns all parts, laid end to end along the dimension named above; an argument that names none is the same for every part. Nothing has to cross between parts.
Inputs may be any that keep to these rules, and one draw needn't show every extreme that they name: `adapter_rank`: ranks are multiples of 8; both 8 and 128 occur in every pool. `request_length`: each row sums to 128.
All inputs are finite; a program needn't handle non-finite values.
Results may differ from the reference program's by a relative error of at most 0.0029.
Values may be sent and summed in bfloat16 or wider, within the bound.
A program may use at most 128 MiB of HBM per device.

```python
import math
import jax
import jax.numpy as jnp
import numpy as np
from jax import lax

D = 8192
OUTW = 1024
RMAX = 128
TOK_DEV = 128
REQ_DEV = 3
ADAPTERS = 128
LONGEST_ROWS = 64
TOKENS = 2048
N_DP = 16


def draw_adapter_rank(key, part):
    key = jax.random.fold_in(key, 11)
    rank_random_key, key_high, key_low = jax.random.split(key, 3)
    drawn = 8 * jax.random.randint(rank_random_key, (ADAPTERS,), 1, RMAX // 8 + 1)
    high_slot = jax.random.randint(key_high, (), 0, ADAPTERS)
    low_slot = (high_slot + 1 + jax.random.randint(key_low, (), 0, ADAPTERS - 1)) % ADAPTERS
    positions = jnp.arange(ADAPTERS)
    drawn = jnp.where(positions == high_slot, RMAX, drawn)
    drawn = jnp.where(positions == low_slot, 8, drawn)
    return drawn.astype(jnp.int32)


def place_ends(array, own_key, low, high):
    index_at = [jax.random.randint(jax.random.fold_in(own_key, axis), (), 0, length) for axis, length in enumerate(array.shape)]
    main_axis = array.shape.index(max(array.shape))
    next_to = index_at[:main_axis] + [(index_at[main_axis] + 1) % array.shape[main_axis]] + index_at[main_axis + 1:]
    return array.at[tuple(index_at)].set(low).at[tuple(next_to)].set(high)


def levels(stream_key, shape, cuts, low, largest):
    def one(position, parts):
        heights = jax.random.uniform(jax.random.fold_in(jax.random.fold_in(stream_key, 6), position), (parts,), jnp.float32, low / len(cuts), largest / len(cuts))
        return jnp.repeat(jnp.exp(heights), shape[position] // parts).reshape((-1,) + (1,) * (len(shape) - position - 1))

    loudness = one(*cuts[0])
    for cut in cuts[1:]:
        loudness = loudness * one(*cut)
    return loudness


def rank_table(amount, skew):
    portions = [(1 << 20) // math.isqrt(grade ** skew) + 1 for grade in range(1, amount + 1)]
    scale = 1 + sum(portions) // (1 << 30)
    return np.cumsum(np.array([max(1, weight // scale) for weight in portions]))


def skewed_ids(stream_key, extent, number_of, skew):
    grid = rank_table(number_of, skew)
    pick = jax.random.randint(jax.random.fold_in(stream_key, 1), extent, 0, int(grid[number_of - 1]))
    standing = jnp.searchsorted(jnp.asarray(grid, jnp.int32), pick, side="right")
    return jax.random.permutation(jax.random.fold_in(stream_key, 2), number_of)[standing].astype(jnp.int32)


def split_up(count, total, limit, lean):
    loads = [(1 << 20) // math.isqrt(standing ** lean) + 1 for standing in range(2, count + 1)]
    spare, counts = total - limit - (count - 1), [1] * (count - 1)
    while spare > 0:
        movable = [i for i in range(count - 1) if counts[i] < limit]
        mass, remaining = sum([loads[i] for i in movable]), spare
        for i in movable:
            addition = min(limit - counts[i], max(1, remaining * loads[i] // mass), spare)
            counts[i] = counts[i] + addition
            spare = spare - addition
    return np.array([limit] + counts)


def uneven_parts(stream_key, number_of, total, reach, skew):
    if number_of == 2:
        one = jax.random.randint(stream_key, (), max(1, total - reach), min(reach, total - 1) + 1)
        return jnp.stack([one, total - one])
    lengths = jnp.asarray(split_up(number_of, total, reach, skew), jnp.int32)
    couples = (number_of - 1) // 2
    giver, receiver = lengths[1:1 + 2 * couples:2], lengths[2:2 + 2 * couples:2]
    room = jnp.minimum(giver - 1, reach - receiver)
    moved = jax.random.randint(jax.random.fold_in(stream_key, 1), (couples,), 0, 1 << 20) % (room + 1)
    lengths = lengths.at[1:1 + 2 * couples:2].set(giver - moved).at[2:2 + 2 * couples:2].set(receiver + moved)
    return lengths[jax.random.permutation(jax.random.fold_in(stream_key, 2), number_of)]


def gaussian(own_key, extent, width, bound, cuts=(), kind=jnp.bfloat16):
    array = width * jax.random.normal(own_key, extent, jnp.float32)
    if cuts:
        array = array * levels(own_key, extent, cuts, -0.22, 0.18)
    return jnp.clip(array, -bound, bound).astype(kind)


def setup_inputs(seed: int = 0, part: int = 0) -> dict:
    key_list = jax.random.split(jax.random.key(seed), 8)
    own_keys = jax.random.split(jax.random.fold_in(key_list[7], part), 8)
    tokens = gaussian(own_keys[0], (TOKENS, D), 1.0, 6.0, ((0, 16),))
    frozen_projection_weight = gaussian(key_list[1], (D, OUTW), D ** -0.5, 0.0625)
    adapter_down = gaussian(own_keys[2], (ADAPTERS, D, RMAX), D ** -0.5, 0.0625, ((1, 16),))
    adapter_up = gaussian(own_keys[3], (ADAPTERS, RMAX, OUTW), RMAX ** -0.5, 0.5, ((1, 16),))
    adapter_rank = draw_adapter_rank(jax.random.fold_in(jax.random.fold_in(key_list[7], part), 71), part)
    request_adapter = place_ends(skewed_ids(own_keys[5], (N_DP, REQ_DEV), ADAPTERS, 2), jax.random.fold_in(own_keys[5], 3), 0, ADAPTERS - 1).astype(jnp.int32)
    request_length = jax.vmap(lambda own: uneven_parts(own, REQ_DEV, TOK_DEV, LONGEST_ROWS, 2))(jax.random.split(own_keys[6], N_DP)).reshape((N_DP, REQ_DEV)).astype(jnp.int32)
    return {"tokens": tokens, "frozen_projection_weight": frozen_projection_weight, "adapter_down": adapter_down, "adapter_up": adapter_up, "adapter_rank": adapter_rank, "request_adapter": request_adapter, "request_length": request_length}


adapter_alpha_scale = 32.0


def row_requests(request_length):
    request_ends = jnp.cumsum(request_length, axis=1)
    block_rows = jnp.arange(TOK_DEV, dtype=jnp.int32)
    return jnp.sum((block_rows[None, :, None] >= request_ends[:, None, :]).astype(jnp.int32), axis=2)


def project_rows(block_rows, row_request, frozen_projection_weight, down_panels, up_panels, adapter_ranks):
    base_rows = jnp.dot(block_rows, frozen_projection_weight, preferred_element_type=jnp.float32)
    onehot = row_request[:, None] == jnp.arange(REQ_DEV, dtype=jnp.int32)[None, :]
    shrunk_all = jnp.einsum("td,qdr->tqr", block_rows.astype(jnp.float32), down_panels.astype(jnp.float32))
    shrunk = jnp.sum(jnp.where(onehot[:, :, None], shrunk_all, jnp.float32(0.0)), axis=1)
    rank_of_row = jnp.sum(jnp.where(onehot, adapter_ranks[None, :], 0), axis=1)
    within = jnp.arange(RMAX, dtype=jnp.int32)[None, :] < rank_of_row[:, None]
    scaling_factor = adapter_alpha_scale / rank_of_row.astype(jnp.float32)
    scaled = jnp.where(within, shrunk * scaling_factor[:, None], jnp.float32(0.0)).astype(jnp.bfloat16)
    placed = jnp.where(onehot[:, :, None], scaled[:, None, :], jnp.zeros((), jnp.bfloat16))
    placed = placed.reshape(TOK_DEV, REQ_DEV * RMAX)
    adapter_term = jnp.dot(placed, up_panels.reshape(REQ_DEV * RMAX, OUTW), preferred_element_type=jnp.float32)
    return (base_rows + adapter_term).astype(jnp.bfloat16)


def reference(tokens, frozen_projection_weight, adapter_down, adapter_up, adapter_rank, request_adapter, request_length):
    row_request = row_requests(request_length)

    def one_device(packed):
        block_rows, adapter_ids, picks = packed
        return project_rows(block_rows, picks, frozen_projection_weight, adapter_down[adapter_ids], adapter_up[adapter_ids], adapter_rank[adapter_ids])

    blocks = tokens.reshape(N_DP, TOK_DEV, D)
    result = lax.map(one_device, (blocks, request_adapter, row_request))
    return result.reshape(TOKENS, OUTW)
```

```python
import functools

import jax
import jax.numpy as jnp
import numpy as np
from jax import lax
from jax.experimental import pallas as pl
from jax.experimental.pallas import tpu as pltpu
from jax.sharding import PartitionSpec as P

MESH = pl.DeviceIdType.MESH


RMAX = 128
TOK_DEV = 128
REQ_DEV = 3


adapter_alpha_scale = 32.0


def row_requests(request_length):
    request_ends = jnp.cumsum(request_length, axis=1)
    block_rows = jnp.arange(TOK_DEV, dtype=jnp.int32)
    return jnp.sum(
        (block_rows[None, :, None] >= request_ends[:, None, :]).astype(jnp.int32), axis=2
    )


def finish_rows(base_rows, shrunk, onehot, adapter_ranks, up_panels):
    rank_of_row = jnp.sum(jnp.where(onehot, adapter_ranks[None, :], 0), axis=1)
    within = jnp.arange(RMAX, dtype=jnp.int32)[None, :] < rank_of_row[:, None]
    scaling_factor = adapter_alpha_scale / rank_of_row.astype(jnp.float32)
    scaled = jnp.where(within, shrunk * scaling_factor[:, None], jnp.float32(0.0)).astype(
        jnp.bfloat16
    )
    placed = jnp.where(onehot[:, :, None], scaled[:, None, :], jnp.zeros((), jnp.bfloat16))
    placed = placed.reshape(TOK_DEV, REQ_DEV * RMAX)
    adapter_term = jnp.dot(
        placed, up_panels.reshape(REQ_DEV * RMAX, -1), preferred_element_type=jnp.float32
    )
    return (base_rows + adapter_term).astype(jnp.bfloat16)


def local(
    tokens,
    frozen_projection_weight,
    adapter_down,
    adapter_up,
    adapter_rank,
    request_adapter,
    request_length,
):
    position = lax.axis_index("dp")
    adapter_ids = lax.dynamic_index_in_dim(request_adapter, position, 0, keepdims=False)
    own_lengths = lax.dynamic_index_in_dim(request_length, position, 0, keepdims=False)
    own_ends = jnp.cumsum(own_lengths)
    row_request = jnp.sum(
        (jnp.arange(TOK_DEV, dtype=jnp.int32)[:, None] >= own_ends[None, :]).astype(jnp.int32),
        axis=1,
    )
    onehot = row_request[:, None] == jnp.arange(REQ_DEV, dtype=jnp.int32)[None, :]
    adapter_ranks = jnp.take(adapter_rank, adapter_ids)
    expected_output = request_adapter.T
    columns = lax.all_to_all(tokens, "dp", split_axis=1, concat_axis=0, tiled=True)
    all_requests = row_requests(request_length)
    base_rows = jnp.dot(tokens, frozen_projection_weight, preferred_element_type=jnp.float32)
    block_count = lax.axis_size("dp") * TOK_DEV // TOK_DEV
    row_block = columns
    row_block = row_block.reshape(block_count, TOK_DEV, row_block.shape[1])

    def add_request(request, running):
        panel_rows = jnp.take(adapter_down, jnp.take(request_adapter, request, axis=1), axis=0)
        product = jnp.einsum(
            "ntc,ncr->ntr", row_block, panel_rows, preferred_element_type=jnp.float32
        )
        return running + jnp.where((all_requests == request)[:, :, None], product, jnp.float32(0.0))

    running = lax.fori_loop(
        0, REQ_DEV, add_request, jnp.zeros((block_count, TOK_DEV, RMAX), jnp.float32)
    )
    shrunk = lax.psum_scatter(
        running.reshape(lax.axis_size("dp") * TOK_DEV, RMAX), "dp", scatter_dimension=0, tiled=True
    )
    up_out = jnp.take(adapter_up, expected_output, axis=0)
    up_panels = lax.all_to_all(up_out, "dp", split_axis=1, concat_axis=1, tiled=True)
    up_panels = up_panels.reshape(REQ_DEV, RMAX, -1)
    return finish_rows(base_rows, shrunk, onehot, adapter_ranks, up_panels)


def flip(me, step, n):
    total, weight = 0, 1
    while weight < n:
        total = total + weight * ((me // weight + step // weight) % 2)
        weight *= 2
    return total


def fused(
    n, req, spread,
    adapters, lengths, ranks, tokens, weight, down, up, place, code,
    out,
    tok, wgt, dwn, upv, placev, codev, base, tok_in, up_out, up_in, part, got1, got2, got3,
    load_sem, wgt_sem, tok_send, tok_recv, up_send, up_recv,
    s1_send, s1_recv, s2_send, s2_recv, s3_send, s3_recv,
):
    me = lax.axis_index("dp")
    rows, width = tokens.shape
    chunk = width // n
    rank_rows = up.shape[1]
    half = up.shape[2] // 2

    loads = [
        pltpu.make_async_copy(up, upv, load_sem.at[0]),
        pltpu.make_async_copy(tokens, tok, load_sem.at[1]),
        pltpu.make_async_copy(down, dwn, load_sem.at[2]),
        pltpu.make_async_copy(place, placev, load_sem.at[3]),
        pltpu.make_async_copy(code, codev, load_sem.at[4]),
    ]

    def weight_copy(c):
        piece = pl.ds(pl.multiple_of(c * chunk, chunk), chunk)
        return pltpu.make_async_copy(weight.at[piece], wgt.at[piece], wgt_sem.at[c])

    def token_copy(step):
        peer = flip(me, step, n)
        return pltpu.make_async_remote_copy(
            src_ref=tokens.at[:, pl.ds(pl.multiple_of(peer * chunk, chunk), chunk)],
            dst_ref=tok_in.at[step],
            send_sem=tok_send.at[step], recv_sem=tok_recv.at[step],
            device_id={"dp": peer}, device_id_type=MESH,
        )

    def up_copy(step):
        peer = flip(me, step, n)
        return pltpu.make_async_remote_copy(
            src_ref=up_out.at[peer], dst_ref=up_in.at[me],
            send_sem=up_send.at[step], recv_sem=up_recv.at[step],
            device_id={"dp": peer}, device_id_type=MESH,
        )

    def up_arrival(step):
        peer = flip(me, step, n)
        return pltpu.make_async_remote_copy(
            src_ref=up_out.at[peer], dst_ref=up_in.at[peer],
            send_sem=up_send.at[step], recv_sem=up_recv.at[step],
            device_id={"dp": peer}, device_id_type=MESH,
        )

    barrier = pltpu.get_barrier_semaphore()

    def greet(step, carry):
        pl.semaphore_signal(barrier, inc=1, device_id={"dp": flip(me, step, n)}, device_id_type=MESH)
        return carry

    lax.fori_loop(1, n, greet, 0)
    loads[0].start()
    loads[1].start()

    def start_weight(c, carry):
        weight_copy(c).start()
        return carry

    lax.fori_loop(0, n, start_weight, 0)
    for load in loads[2:]:
        load.start()
    pl.semaphore_wait(barrier, n - 1)

    def send_tokens(i, carry):
        token_copy(n - 1 - i).start()
        return carry

    lax.fori_loop(0, n - 1, send_tokens, 0)

    loads[0].wait()

    def pick_up(i, carry):
        panels = [upv[adapters[i, q]].astype(jnp.float32) for q in range(req)]
        picked = [p[:, h * half:(h + 1) * half] for h in range(2) for p in panels]
        up_out[i] = jnp.concatenate(picked, axis=0).astype(jnp.bfloat16)
        return carry

    lax.fori_loop(0, n, pick_up, 0)
    up_in[me] = up_out[me]

    def send_up(i, carry):
        up_copy(n - 1 - i).start()
        return carry

    lax.fori_loop(0, n - 1, send_up, 0)

    loads[1].wait()
    base[...] = jnp.zeros_like(base)

    def add_base(c, carry):
        weight_copy(c).wait()
        piece = pl.ds(pl.multiple_of(c * chunk, chunk), chunk)
        base[...] += jnp.dot(tok[:, piece], wgt[piece, :], preferred_element_type=jnp.float32)
        return carry

    lax.fori_loop(0, n, add_base, 0)
    for load in loads[2:]:
        load.wait()
    tok_in[0] = tok[:, pl.ds(pl.multiple_of(me * chunk, chunk), chunk)]

    row = lax.broadcasted_iota(jnp.int32, (rows, 1), 0)

    def shrink(step):
        i = flip(me, step, n)
        block = tok_in[step]
        total = jnp.dot(block, dwn[adapters[i, 0]], preferred_element_type=jnp.float32)
        end = jnp.int32(0)
        for q in range(1, req):
            end = end + lengths[i, q - 1]
            product = jnp.dot(block, dwn[adapters[i, q]], preferred_element_type=jnp.float32)
            total = jnp.where(row >= end, product, total)
        part[step] = total

    def sum_copy(src, dst, sends, recvs, slot, peer):
        return pltpu.make_async_remote_copy(
            src_ref=src, dst_ref=dst, send_sem=sends.at[slot], recv_sem=recvs.at[slot],
            device_id={"dp": peer}, device_id_type=MESH,
        )

    waiting = []
    for m in range(n // 4):
        def one(step, carry):
            @pl.when(step > 0)
            def _():
                token_copy(step).wait_recv()
            shrink(step)
            return carry

        lax.fori_loop(4 * m, 4 * m + 4, one, 0)
        first = [
            sum_copy(part.at[2 * k + 1], got1.at[k], s1_send, s1_recv, k, flip(me, 1, n))
            for k in (2 * m, 2 * m + 1)
        ]
        for copy in first:
            copy.start()
        for k, copy in zip((2 * m + 1, 2 * m), reversed(first)):
            copy.wait_recv()
            part[2 * k] = part[2 * k] + got1[k]
            if k % 2:
                second = sum_copy(part.at[2 * k], got2.at[m], s2_send, s2_recv, m, flip(me, 2, n))
                second.start()
        second.wait_recv()
        part[4 * m] = part[4 * m] + got2[m]
        waiting += first + [second]
        if m:
            third = sum_copy(part.at[4 * m], got3.at[m], s3_send, s3_recv, m, flip(me, 4 * m, n))
            third.start()
            waiting.append(third)

    shrunk = part[0]
    for m in range(1, n // 4):
        sum_copy(part.at[4 * m], got3.at[m], s3_send, s3_recv, m, flip(me, 4 * m, n)).wait_recv()
        shrunk = shrunk + got3[m]

    request = jnp.zeros((rows, 1), jnp.int32)
    rank = jnp.zeros((rows, 1), jnp.int32) + ranks[adapters[me, 0]]
    end = jnp.int32(0)
    for q in range(1, req):
        end = end + lengths[me, q - 1]
        later = row >= end
        request = jnp.where(later, q, request)
        rank = jnp.where(later, ranks[adapters[me, q]], rank)
    within = lax.broadcasted_iota(jnp.int32, shrunk.shape, 1) < rank
    factor = 32.0 / rank.astype(jnp.float32)
    scaled = jnp.where(within, shrunk * factor, 0.0).astype(jnp.bfloat16)
    spread_out = jnp.dot(scaled, placev[...], preferred_element_type=jnp.float32)
    codes = codev[0:1, :]

    def await_up(step, carry):
        up_arrival(step).wait_recv()
        return carry

    lax.fori_loop(1, n, await_up, 0)
    panels = up_in[...].reshape(spread, half)
    for h in range(2):
        placed = jnp.where(codes == request + h * req, spread_out, 0.0).astype(jnp.bfloat16)
        term = jnp.dot(placed, panels, preferred_element_type=jnp.float32)
        piece = slice(h * half, (h + 1) * half)
        out[:, piece] = (base[:, piece] + term).astype(jnp.bfloat16)

    def await_sent(step, carry):
        token_copy(step).wait_send()
        up_copy(step).wait_send()
        return carry

    lax.fori_loop(1, n, await_sent, 0)
    for copy in waiting:
        copy.wait_send()


def fused_local(tokens, weight, down, up, ranks, adapters, lengths):
    n = lax.axis_size("dp")
    rows, width = tokens.shape
    chunk = width // n
    columns = weight.shape[1]
    req = adapters.shape[1]
    rank_rows, rmax = up.shape[1], down.shape[2]
    half = columns // 2
    group = 2 * req * rank_rows
    spread = n * group
    slot = np.arange(spread)
    rank_of = (slot // group) * rank_rows + slot % rank_rows
    place = jnp.asarray(np.arange(rmax)[:, None] == rank_of[None, :], jnp.bfloat16)
    code = jnp.asarray(np.tile((slot % group) // rank_rows, (8, 1)), jnp.int32)
    dma = pltpu.SemaphoreType.DMA
    smem = pl.BlockSpec(memory_space=pltpu.SMEM)
    hbm = pl.BlockSpec(memory_space=pl.ANY)
    return pl.pallas_call(
        functools.partial(fused, n, req, spread),
        out_shape=jax.ShapeDtypeStruct((rows, columns), jnp.bfloat16),
        in_specs=[smem] * 3 + [hbm] * 6,
        out_specs=pl.BlockSpec(memory_space=pltpu.VMEM),
        scratch_shapes=[
            pltpu.VMEM((rows, width), jnp.bfloat16),
            pltpu.VMEM(weight.shape, jnp.bfloat16),
            pltpu.VMEM(down.shape, jnp.bfloat16),
            pltpu.VMEM(up.shape, jnp.bfloat16),
            pltpu.VMEM(place.shape, jnp.bfloat16),
            pltpu.VMEM(code.shape, jnp.int32),
            pltpu.VMEM((rows, columns), jnp.float32),
            pltpu.VMEM((n, rows, chunk), jnp.bfloat16),
            pltpu.VMEM((n, group, half), jnp.bfloat16),
            pltpu.VMEM((n, group, half), jnp.bfloat16),
            pltpu.VMEM((n, rows, rmax), jnp.float32),
            pltpu.VMEM((n // 2, rows, rmax), jnp.float32),
            pltpu.VMEM((n // 4, rows, rmax), jnp.float32),
            pltpu.VMEM((n // 4, rows, rmax), jnp.float32),
            dma((5,)), dma((n,)), dma((n,)), dma((n,)), dma((n,)), dma((n,)),
            dma((n // 2,)), dma((n // 2,)), dma((n // 4,)), dma((n // 4,)), dma((n // 4,)), dma((n // 4,)),
        ],
        compiler_params=pltpu.CompilerParams(
            collective_id=0, has_side_effects=True, vmem_limit_bytes=56 * 1024 * 1024
        ),
        cost_estimate=pl.CostEstimate(flops=3 * 10**9, bytes_accessed=4 * 10**7, transcendentals=0),
    )(adapters, lengths, ranks, tokens, weight, down, up, place, code)


def fits(mesh, tokens, up):
    n = mesh.shape["dp"]
    chunk, rank_rows = tokens.shape[1] // n, up.shape[1] // n
    return n >= 8 and n & (n - 1) == 0 and n <= 32 and chunk % 128 == 0 and rank_rows % 8 == 0


def solution(mesh):
    in_specs = (
        P(("group", "dp"), None),
        P(),
        P("group", "dp", None),
        P("group", "dp", None),
        P("group"),
        P("group", None),
        P("group", None),
    )
    out_specs = P(("group", "dp"), None)

    def run(*arrays):
        body = fused_local if fits(mesh, arrays[0], arrays[3]) else local
        return jax.shard_map(body, mesh=mesh, in_specs=in_specs, out_specs=out_specs, check_vma=False)(*arrays)

    return run
```

```python
import functools

import jax
import jax.numpy as jnp
import numpy as np
from jax import lax
from jax.experimental import pallas as pl
from jax.experimental.pallas import tpu as pltpu
from jax.sharding import PartitionSpec as P

MESH = pl.DeviceIdType.MESH


RMAX = 128
TOK_DEV = 128
REQ_DEV = 3


adapter_alpha_scale = 32.0


def row_requests(request_length):
    request_ends = jnp.cumsum(request_length, axis=1)
    block_rows = jnp.arange(TOK_DEV, dtype=jnp.int32)
    return jnp.sum(
        (block_rows[None, :, None] >= request_ends[:, None, :]).astype(jnp.int32), axis=2
    )


def finish_rows(base_rows, shrunk, onehot, adapter_ranks, up_panels):
    rank_of_row = jnp.sum(jnp.where(onehot, adapter_ranks[None, :], 0), axis=1)
    within = jnp.arange(RMAX, dtype=jnp.int32)[None, :] < rank_of_row[:, None]
    scaling_factor = adapter_alpha_scale / rank_of_row.astype(jnp.float32)
    scaled = jnp.where(within, shrunk * scaling_factor[:, None], jnp.float32(0.0)).astype(
        jnp.bfloat16
    )
    placed = jnp.where(onehot[:, :, None], scaled[:, None, :], jnp.zeros((), jnp.bfloat16))
    placed = placed.reshape(TOK_DEV, REQ_DEV * RMAX)
    adapter_term = jnp.dot(
        placed, up_panels.reshape(REQ_DEV * RMAX, -1), preferred_element_type=jnp.float32
    )
    return (base_rows + adapter_term).astype(jnp.bfloat16)


def local(
    tokens,
    frozen_projection_weight,
    adapter_down,
    adapter_up,
    adapter_rank,
    request_adapter,
    request_length,
):
    position = lax.axis_index("dp")
    adapter_ids = lax.dynamic_index_in_dim(request_adapter, position, 0, keepdims=False)
    own_lengths = lax.dynamic_index_in_dim(request_length, position, 0, keepdims=False)
    own_ends = jnp.cumsum(own_lengths)
    row_request = jnp.sum(
        (jnp.arange(TOK_DEV, dtype=jnp.int32)[:, None] >= own_ends[None, :]).astype(jnp.int32),
        axis=1,
    )
    onehot = row_request[:, None] == jnp.arange(REQ_DEV, dtype=jnp.int32)[None, :]
    adapter_ranks = jnp.take(adapter_rank, adapter_ids)
    expected_output = request_adapter.T
    columns = lax.all_to_all(tokens, "dp", split_axis=1, concat_axis=0, tiled=True)
    all_requests = row_requests(request_length)
    base_rows = jnp.dot(tokens, frozen_projection_weight, preferred_element_type=jnp.float32)
    block_count = lax.axis_size("dp") * TOK_DEV // TOK_DEV
    row_block = columns
    row_block = row_block.reshape(block_count, TOK_DEV, row_block.shape[1])

    def add_request(request, running):
        panel_rows = jnp.take(adapter_down, jnp.take(request_adapter, request, axis=1), axis=0)
        product = jnp.einsum(
            "ntc,ncr->ntr", row_block, panel_rows, preferred_element_type=jnp.float32
        )
        return running + jnp.where((all_requests == request)[:, :, None], product, jnp.float32(0.0))

    running = lax.fori_loop(
        0, REQ_DEV, add_request, jnp.zeros((block_count, TOK_DEV, RMAX), jnp.float32)
    )
    shrunk = lax.psum_scatter(
        running.reshape(lax.axis_size("dp") * TOK_DEV, RMAX), "dp", scatter_dimension=0, tiled=True
    )
    up_out = jnp.take(adapter_up, expected_output, axis=0)
    up_panels = lax.all_to_all(up_out, "dp", split_axis=1, concat_axis=1, tiled=True)
    up_panels = up_panels.reshape(REQ_DEV, RMAX, -1)
    return finish_rows(base_rows, shrunk, onehot, adapter_ranks, up_panels)


def flip(me, step, n):
    total, weight = 0, 1
    while weight < n:
        total = total + weight * ((me // weight + step // weight) % 2)
        weight *= 2
    return total


AHEAD = 3


def fused(
    n, req,
    adapters_in, lengths_in, ranks_in, tokens, weight, down, up, code,
    out,
    adapters, lengths, ranks, tok, wgt, dwn, upv, codev, base, tok_in, up_out, up_in, part, got,
    load_sem, wgt_sem, tok_send, tok_recv, up_send, up_recv, sum_send, sum_recv,
):
    me = lax.axis_index("dp")
    rows, width = tokens.shape
    chunk = width // n
    far = n // 2
    group, half = up_in.shape[1:]

    loads = [
        pltpu.make_async_copy(source, target, load_sem.at[k])
        for k, (source, target) in enumerate((
            (up, upv), (adapters_in, adapters), (lengths_in, lengths), (ranks_in, ranks),
            (tokens, tok), (down, dwn), (code, codev),
        ))
    ]

    def weight_copy(c):
        piece = pl.ds(pl.multiple_of(c * chunk, chunk), chunk)
        return pltpu.make_async_copy(weight.at[piece], wgt.at[piece], wgt_sem.at[c])

    def token_copy(step):
        peer = flip(me, step, n)
        return pltpu.make_async_remote_copy(
            src_ref=tokens.at[:, pl.ds(pl.multiple_of(peer * chunk, chunk), chunk)],
            dst_ref=tok_in.at[step],
            send_sem=tok_send.at[step], recv_sem=tok_recv.at[step],
            device_id={"dp": peer}, device_id_type=MESH,
        )

    def up_copy(step, arriving=False):
        peer = flip(me, step, n)
        return pltpu.make_async_remote_copy(
            src_ref=up_out.at[peer], dst_ref=up_in.at[peer if arriving else me],
            send_sem=up_send.at[step], recv_sem=up_recv.at[step],
            device_id={"dp": peer}, device_id_type=MESH,
        )

    def sum_copy(level, k):
        slot = n - (n >> level) + k
        return pltpu.make_async_remote_copy(
            src_ref=part.at[(2 * k + 1) << level], dst_ref=got.at[slot],
            send_sem=sum_send.at[slot], recv_sem=sum_recv.at[slot],
            device_id={"dp": flip(me, 1 << level, n)}, device_id_type=MESH,
        )

    barrier = pltpu.get_barrier_semaphore()

    def greet(step, carry):
        pl.semaphore_signal(barrier, inc=1, device_id={"dp": flip(me, step, n)}, device_id_type=MESH)
        return carry

    lax.fori_loop(1, n, greet, 0)
    for load in loads:
        load.start()

    def start_weight(c, carry):
        weight_copy(c).start()
        return carry

    lax.fori_loop(0, n, start_weight, 0)
    pl.semaphore_wait(barrier, n - 1)
    for t in range(AHEAD):
        token_copy(far + t).start()
        if t:
            token_copy(t).start()

    for load in loads[:4]:
        load.wait()

    def pick_up(i, carry):
        panels = [upv[adapters[q, i]].astype(jnp.float32) for q in range(req)]
        picked = [p[:, h * half:(h + 1) * half] for h in range(2) for p in panels]
        up_out[i] = jnp.concatenate(picked, axis=0).astype(jnp.bfloat16)
        return carry

    lax.fori_loop(0, n, pick_up, 0)
    up_in[me] = up_out[me]

    row = lax.broadcasted_iota(jnp.int32, (rows, 1), 0)

    def shrink(step):
        i = flip(me, step, n)
        block = tok_in[step]
        total = jnp.dot(block, dwn[adapters[0, i]], preferred_element_type=jnp.float32)
        end = jnp.int32(0)
        for q in range(1, req):
            end = end + lengths[q - 1, i]
            product = jnp.dot(block, dwn[adapters[q, i]], preferred_element_type=jnp.float32)
            total = jnp.where(row >= end, product, total)
        part[step] = total

    def add_base(c, carry):
        weight_copy(c).wait()
        piece = pl.ds(pl.multiple_of(c * chunk, chunk), chunk)
        base[...] += jnp.dot(tok[:, piece], wgt[piece, :], preferred_element_type=jnp.float32)
        return carry

    ready, moving, sent = set(), [], []

    def mark(level, block):
        ready.add((level, block))
        k = block // 2
        if (1 << level) < n and {(level, 2 * k), (level, 2 * k + 1)} <= ready:
            sum_copy(level, k).start()
            moving.append((level, k))
            sent.append((level, k))

    def absorb():
        level, k = moving.pop(0)
        sum_copy(level, k).wait_recv()
        kept = (2 * k) << level
        part[kept] = part[kept] + got[n - (n >> level) + k]
        mark(level + 1, k)

    ups = list(range(far, n))
    for t in range(far):
        for _ in range(len(moving)):
            absorb()
        if t == 0:
            for load in loads[4:]:
                load.wait()
            tok_in[0] = tok[:, pl.ds(pl.multiple_of(me * chunk, chunk), chunk)]
            base[...] = jnp.zeros_like(base)
        else:
            up_copy(t).start()
            token_copy(t).wait_recv()
        if t + AHEAD < far:
            token_copy(t + AHEAD).start()
        lax.fori_loop(2 * t, 2 * t + 2, add_base, 0)
        token_copy(far + t).wait_recv()
        if t + AHEAD < far:
            token_copy(far + t + AHEAD).start()
        else:
            for step in ups if t == far - 1 else ups[:2]:
                up_copy(step).start()
            ups = ups[2:]

        def one(u, carry):
            shrink(t + u * far)
            return carry

        lax.fori_loop(0, 2, one, 0)
        mark(0, t)
        mark(0, far + t)
    while moving:
        absorb()
    shrunk = part[0]

    request = jnp.zeros((rows, 1), jnp.int32)
    rank = jnp.zeros((rows, 1), jnp.int32) + ranks[adapters[0, me]]
    end = jnp.int32(0)
    for q in range(1, req):
        end = end + lengths[q - 1, me]
        later = row >= end
        request = jnp.where(later, q, request)
        rank = jnp.where(later, ranks[adapters[q, me]], rank)
    within = lax.broadcasted_iota(jnp.int32, shrunk.shape, 1) < rank
    factor = 32.0 / rank.astype(jnp.float32)
    scaled = jnp.where(within, shrunk * factor, 0.0).astype(jnp.bfloat16)
    span = far * group
    codes = codev[0:1, 0:span]
    rank_index = lax.broadcasted_iota(jnp.int32, (shrunk.shape[1], span), 0)

    def await_up(step, carry):
        up_copy(step, arriving=True).wait_recv()
        return carry

    near_side = me // far
    for side, steps in ((near_side, (1, far)), (1 - near_side, (far, n))):
        rank_of = codev[1:2, pl.ds(pl.multiple_of(side * span, span), span)]
        picked = jnp.where(rank_index == rank_of, 1.0, 0.0).astype(jnp.bfloat16)
        spread_out = jnp.dot(scaled, picked, preferred_element_type=jnp.float32)
        placed = [
            jnp.where(codes == request + h * req, spread_out, 0.0).astype(jnp.bfloat16) for h in range(2)
        ]
        lax.fori_loop(*steps, await_up, 0)
        panels = up_in[pl.ds(side * far, far)].reshape(span, half)
        for h in range(2):
            piece = slice(h * half, (h + 1) * half)
            total = base[:, piece] + jnp.dot(placed[h], panels, preferred_element_type=jnp.float32)
            if steps[0] == 1:
                base[:, piece] = total
            else:
                out[:, piece] = total.astype(jnp.bfloat16)

    def await_sent(step, carry):
        token_copy(step).wait_send()
        up_copy(step).wait_send()
        return carry

    lax.fori_loop(1, n, await_sent, 0)
    for pair in sent:
        sum_copy(*pair).wait_send()


def fused_local(tokens, weight, down, up, ranks, adapters, lengths):
    n = lax.axis_size("dp")
    rows, width = tokens.shape
    chunk = width // n
    columns = weight.shape[1]
    req = adapters.shape[1]
    rank_rows, rmax = up.shape[1], down.shape[2]
    half = columns // 2
    group = 2 * req * rank_rows
    spread = n * group
    slot = np.arange(spread)
    rank_of = (slot // group) * rank_rows + slot % rank_rows
    code = np.zeros((8, spread), np.int32)
    code[0], code[1] = (slot % group) // rank_rows, rank_of
    code = jnp.asarray(code)
    dma = pltpu.SemaphoreType.DMA
    return pl.pallas_call(
        functools.partial(fused, n, req),
        out_shape=jax.ShapeDtypeStruct((rows, columns), jnp.bfloat16),
        in_specs=[pl.BlockSpec(memory_space=pl.ANY)] * 8,
        out_specs=pl.BlockSpec(memory_space=pltpu.VMEM),
        scratch_shapes=[
            pltpu.SMEM(adapters.shape[::-1], jnp.int32),
            pltpu.SMEM(lengths.shape[::-1], jnp.int32),
            pltpu.SMEM(ranks.shape, jnp.int32),
            pltpu.VMEM((rows, width), jnp.bfloat16),
            pltpu.VMEM(weight.shape, jnp.bfloat16),
            pltpu.VMEM(down.shape, jnp.bfloat16),
            pltpu.VMEM(up.shape, jnp.bfloat16),
            pltpu.VMEM(code.shape, jnp.int32),
            pltpu.VMEM((rows, columns), jnp.float32),
            pltpu.VMEM((n, rows, chunk), jnp.bfloat16),
            pltpu.VMEM((n, group, half), jnp.bfloat16),
            pltpu.VMEM((n, group, half), jnp.bfloat16),
            pltpu.VMEM((n, rows, rmax), jnp.float32),
            pltpu.VMEM((n - 1, rows, rmax), jnp.float32),
            dma((7,)), dma((n,)), dma((n,)), dma((n,)), dma((n,)), dma((n,)), dma((n,)), dma((n,)),
        ],
        compiler_params=pltpu.CompilerParams(
            collective_id=0, has_side_effects=True, vmem_limit_bytes=56 * 1024 * 1024
        ),
        cost_estimate=pl.CostEstimate(flops=3 * 10**9, bytes_accessed=4 * 10**7, transcendentals=0),
    )(adapters.T, lengths.T, ranks, tokens, weight, down, up, code)


def fits(mesh, tokens, up):
    n = mesh.shape["dp"]
    chunk, rank_rows = tokens.shape[1] // n, up.shape[1] // n
    return n >= 8 and n & (n - 1) == 0 and n <= 32 and chunk % 128 == 0 and rank_rows % 8 == 0


def solution(mesh):
    in_specs = (
        P(("group", "dp"), None),
        P(),
        P("group", "dp", None),
        P("group", "dp", None),
        P("group"),
        P("group", None),
        P("group", None),
    )
    out_specs = P(("group", "dp"), None)

    def run(*arrays):
        body = fused_local if fits(mesh, arrays[0], arrays[3]) else local
        return jax.shard_map(body, mesh=mesh, in_specs=in_specs, out_specs=out_specs, check_vma=False)(*arrays)

    return run
```

```python
import functools

import jax
import jax.numpy as jnp
import numpy as np
from jax import lax
from jax.experimental import pallas as pl
from jax.experimental.pallas import tpu as pltpu
from jax.sharding import PartitionSpec as P

MESH = pl.DeviceIdType.MESH


RMAX = 128
TOK_DEV = 128
REQ_DEV = 3


adapter_alpha_scale = 32.0


def row_requests(request_length):
    request_ends = jnp.cumsum(request_length, axis=1)
    block_rows = jnp.arange(TOK_DEV, dtype=jnp.int32)
    return jnp.sum(
        (block_rows[None, :, None] >= request_ends[:, None, :]).astype(jnp.int32), axis=2
    )


def finish_rows(base_rows, shrunk, onehot, adapter_ranks, up_panels):
    rank_of_row = jnp.sum(jnp.where(onehot, adapter_ranks[None, :], 0), axis=1)
    within = jnp.arange(RMAX, dtype=jnp.int32)[None, :] < rank_of_row[:, None]
    scaling_factor = adapter_alpha_scale / rank_of_row.astype(jnp.float32)
    scaled = jnp.where(within, shrunk * scaling_factor[:, None], jnp.float32(0.0)).astype(
        jnp.bfloat16
    )
    placed = jnp.where(onehot[:, :, None], scaled[:, None, :], jnp.zeros((), jnp.bfloat16))
    placed = placed.reshape(TOK_DEV, REQ_DEV * RMAX)
    adapter_term = jnp.dot(
        placed, up_panels.reshape(REQ_DEV * RMAX, -1), preferred_element_type=jnp.float32
    )
    return (base_rows + adapter_term).astype(jnp.bfloat16)


def local(
    tokens,
    frozen_projection_weight,
    adapter_down,
    adapter_up,
    adapter_rank,
    request_adapter,
    request_length,
):
    position = lax.axis_index("dp")
    adapter_ids = lax.dynamic_index_in_dim(request_adapter, position, 0, keepdims=False)
    own_lengths = lax.dynamic_index_in_dim(request_length, position, 0, keepdims=False)
    own_ends = jnp.cumsum(own_lengths)
    row_request = jnp.sum(
        (jnp.arange(TOK_DEV, dtype=jnp.int32)[:, None] >= own_ends[None, :]).astype(jnp.int32),
        axis=1,
    )
    onehot = row_request[:, None] == jnp.arange(REQ_DEV, dtype=jnp.int32)[None, :]
    adapter_ranks = jnp.take(adapter_rank, adapter_ids)
    expected_output = request_adapter.T
    columns = lax.all_to_all(tokens, "dp", split_axis=1, concat_axis=0, tiled=True)
    all_requests = row_requests(request_length)
    base_rows = jnp.dot(tokens, frozen_projection_weight, preferred_element_type=jnp.float32)
    block_count = lax.axis_size("dp") * TOK_DEV // TOK_DEV
    row_block = columns
    row_block = row_block.reshape(block_count, TOK_DEV, row_block.shape[1])

    def add_request(request, running):
        panel_rows = jnp.take(adapter_down, jnp.take(request_adapter, request, axis=1), axis=0)
        product = jnp.einsum(
            "ntc,ncr->ntr", row_block, panel_rows, preferred_element_type=jnp.float32
        )
        return running + jnp.where((all_requests == request)[:, :, None], product, jnp.float32(0.0))

    running = lax.fori_loop(
        0, REQ_DEV, add_request, jnp.zeros((block_count, TOK_DEV, RMAX), jnp.float32)
    )
    shrunk = lax.psum_scatter(
        running.reshape(lax.axis_size("dp") * TOK_DEV, RMAX), "dp", scatter_dimension=0, tiled=True
    )
    up_out = jnp.take(adapter_up, expected_output, axis=0)
    up_panels = lax.all_to_all(up_out, "dp", split_axis=1, concat_axis=1, tiled=True)
    up_panels = up_panels.reshape(REQ_DEV, RMAX, -1)
    return finish_rows(base_rows, shrunk, onehot, adapter_ranks, up_panels)


def flip(me, step, n):
    total, weight = 0, 1
    while weight < n:
        total = total + weight * ((me // weight + step // weight) % 2)
        weight *= 2
    return total


AHEAD = 2


def fused(
    n, req,
    adapters_in, lengths_in, ranks_in, tokens, weight, down, up, code,
    out,
    adapters, lengths, ranks, tok, wgt, dwn, upv, codev, base, tok_in, up_out, up_in, part, got,
    load_sem, wgt_sem, tok_send, tok_recv, up_send, up_recv, sum_send, sum_recv,
):
    me = lax.axis_index("dp")
    rows, width = tokens.shape
    chunk = width // n
    far = n // 2
    group, half = up_in.shape[1:]

    loads = [
        pltpu.make_async_copy(source, target, load_sem.at[k])
        for k, (source, target) in enumerate((
            (up, upv), (adapters_in, adapters), (lengths_in, lengths), (ranks_in, ranks),
            (tokens, tok), (down, dwn), (code, codev),
        ))
    ]

    def weight_copy(c):
        piece = pl.ds(pl.multiple_of(c * chunk, chunk), chunk)
        return pltpu.make_async_copy(weight.at[piece], wgt.at[piece], wgt_sem.at[c])

    def token_copy(step):
        peer = flip(me, step, n)
        return pltpu.make_async_remote_copy(
            src_ref=tokens.at[:, pl.ds(pl.multiple_of(peer * chunk, chunk), chunk)],
            dst_ref=tok_in.at[step],
            send_sem=tok_send.at[step], recv_sem=tok_recv.at[step],
            device_id={"dp": peer}, device_id_type=MESH,
        )

    def up_copy(step, arriving=False):
        peer = flip(me, step, n)
        return pltpu.make_async_remote_copy(
            src_ref=up_out.at[peer], dst_ref=up_in.at[peer if arriving else me],
            send_sem=up_send.at[step], recv_sem=up_recv.at[step],
            device_id={"dp": peer}, device_id_type=MESH,
        )

    def sum_copy(level, k):
        slot = n - (n >> level) + k
        return pltpu.make_async_remote_copy(
            src_ref=part.at[(2 * k + 1) << level], dst_ref=got.at[slot],
            send_sem=sum_send.at[slot], recv_sem=sum_recv.at[slot],
            device_id={"dp": flip(me, 1 << level, n)}, device_id_type=MESH,
        )

    barrier = pltpu.get_barrier_semaphore()

    def greet(step, carry):
        pl.semaphore_signal(barrier, inc=1, device_id={"dp": flip(me, step, n)}, device_id_type=MESH)
        return carry

    lax.fori_loop(1, n, greet, 0)
    for load in loads:
        load.start()

    def start_weight(c, carry):
        weight_copy(c).start()
        return carry

    lax.fori_loop(0, n, start_weight, 0)
    pl.semaphore_wait(barrier, n - 1)
    for t in range(AHEAD):
        token_copy(far + t).start()
        for step in (2 * t, 2 * t + 1):
            if step:
                token_copy(step).start()

    for load in loads[:4]:
        load.wait()

    def pick_up(i, carry):
        panels = [upv[adapters[q, i]].astype(jnp.float32) for q in range(req)]
        picked = [p[:, h * half:(h + 1) * half] for h in range(2) for p in panels]
        up_out[i] = jnp.concatenate(picked, axis=0).astype(jnp.bfloat16)
        return carry

    lax.fori_loop(0, n, pick_up, 0)
    up_in[me] = up_out[me]

    row = lax.broadcasted_iota(jnp.int32, (rows, 1), 0)

    def shrink(step):
        i = flip(me, step, n)
        block = tok_in[step]
        total = jnp.dot(block, dwn[adapters[0, i]], preferred_element_type=jnp.float32)
        end = jnp.int32(0)
        for q in range(1, req):
            end = end + lengths[q - 1, i]
            product = jnp.dot(block, dwn[adapters[q, i]], preferred_element_type=jnp.float32)
            total = jnp.where(row >= end, product, total)
        part[step] = total

    def add_base(c, carry):
        weight_copy(c).wait()
        piece = pl.ds(pl.multiple_of(c * chunk, chunk), chunk)
        base[...] += jnp.dot(tok[:, piece], wgt[piece, :], preferred_element_type=jnp.float32)
        return carry

    ready, moving, sent = set(), [], []

    def mark(level, block):
        ready.add((level, block))
        k = block // 2
        if (1 << level) < n and {(level, 2 * k), (level, 2 * k + 1)} <= ready:
            sum_copy(level, k).start()
            moving.append((level, k))
            sent.append((level, k))

    def absorb():
        level, k = moving.pop(0)
        sum_copy(level, k).wait_recv()
        kept = (2 * k) << level
        part[kept] = part[kept] + got[n - (n >> level) + k]
        mark(level + 1, k)

    ups = list(range(far, n))

    def start_ups(count):
        for step in ups[:count]:
            up_copy(step).start()
        del ups[:count]

    for t in range(far):
        near = [step for step in (2 * t, 2 * t + 1) if step < far]
        for _ in range(len(moving)):
            absorb()
        if t == 0:
            for load in loads[4:]:
                load.wait()
            tok_in[0] = tok[:, pl.ds(pl.multiple_of(me * chunk, chunk), chunk)]
            base[...] = jnp.zeros_like(base)
        for step in near:
            if step:
                token_copy(step).wait_recv()
            if step + 2 * AHEAD < far:
                token_copy(step + 2 * AHEAD).start()
        if t:
            up_copy(t).start()
        lax.fori_loop(2 * t, 2 * t + 2, add_base, 0)
        if near:
            def one(step, carry):
                shrink(step)
                return carry

            lax.fori_loop(near[0], near[-1] + 1, one, 0)
            for step in near:
                mark(0, step)
        token_copy(far + t).wait_recv()
        if t + AHEAD < far:
            token_copy(far + t + AHEAD).start()
        else:
            start_ups(t + AHEAD + 1 - far)
        shrink(far + t)
        mark(0, far + t)
    start_ups(2)
    while moving:
        absorb()
        start_ups(2)
    start_ups(n)
    shrunk = part[0]

    request = jnp.zeros((rows, 1), jnp.int32)
    rank = jnp.zeros((rows, 1), jnp.int32) + ranks[adapters[0, me]]
    end = jnp.int32(0)
    for q in range(1, req):
        end = end + lengths[q - 1, me]
        later = row >= end
        request = jnp.where(later, q, request)
        rank = jnp.where(later, ranks[adapters[q, me]], rank)
    within = lax.broadcasted_iota(jnp.int32, shrunk.shape, 1) < rank
    factor = 32.0 / rank.astype(jnp.float32)
    scaled = jnp.where(within, shrunk * factor, 0.0).astype(jnp.bfloat16)
    span = far * group
    codes = codev[0:1, 0:span]
    rank_index = lax.broadcasted_iota(jnp.int32, (shrunk.shape[1], span), 0)

    def await_up(step, carry):
        up_copy(step, arriving=True).wait_recv()
        return carry

    near_side = me // far
    for side, steps in ((near_side, (1, far)), (1 - near_side, (far, n))):
        rank_of = codev[1:2, pl.ds(pl.multiple_of(side * span, span), span)]
        picked = jnp.where(rank_index == rank_of, 1.0, 0.0).astype(jnp.bfloat16)
        spread_out = jnp.dot(scaled, picked, preferred_element_type=jnp.float32)
        placed = [
            jnp.where(codes == request + h * req, spread_out, 0.0).astype(jnp.bfloat16) for h in range(2)
        ]
        lax.fori_loop(*steps, await_up, 0)
        panels = up_in[pl.ds(side * far, far)].reshape(span, half)
        for h in range(2):
            piece = slice(h * half, (h + 1) * half)
            total = base[:, piece] + jnp.dot(placed[h], panels, preferred_element_type=jnp.float32)
            if steps[0] == 1:
                base[:, piece] = total
            else:
                out[:, piece] = total.astype(jnp.bfloat16)

    def await_sent(step, carry):
        token_copy(step).wait_send()
        up_copy(step).wait_send()
        return carry

    lax.fori_loop(1, n, await_sent, 0)
    for pair in sent:
        sum_copy(*pair).wait_send()


def fused_local(tokens, weight, down, up, ranks, adapters, lengths):
    n = lax.axis_size("dp")
    rows, width = tokens.shape
    chunk = width // n
    columns = weight.shape[1]
    req = adapters.shape[1]
    rank_rows, rmax = up.shape[1], down.shape[2]
    half = columns // 2
    group = 2 * req * rank_rows
    spread = n * group
    slot = np.arange(spread)
    rank_of = (slot // group) * rank_rows + slot % rank_rows
    code = np.zeros((8, spread), np.int32)
    code[0], code[1] = (slot % group) // rank_rows, rank_of
    code = jnp.asarray(code)
    dma = pltpu.SemaphoreType.DMA
    return pl.pallas_call(
        functools.partial(fused, n, req),
        out_shape=jax.ShapeDtypeStruct((rows, columns), jnp.bfloat16),
        in_specs=[pl.BlockSpec(memory_space=pl.ANY)] * 8,
        out_specs=pl.BlockSpec(memory_space=pltpu.VMEM),
        scratch_shapes=[
            pltpu.SMEM(adapters.shape[::-1], jnp.int32),
            pltpu.SMEM(lengths.shape[::-1], jnp.int32),
            pltpu.SMEM(ranks.shape, jnp.int32),
            pltpu.VMEM((rows, width), jnp.bfloat16),
            pltpu.VMEM(weight.shape, jnp.bfloat16),
            pltpu.VMEM(down.shape, jnp.bfloat16),
            pltpu.VMEM(up.shape, jnp.bfloat16),
            pltpu.VMEM(code.shape, jnp.int32),
            pltpu.VMEM((rows, columns), jnp.float32),
            pltpu.VMEM((n, rows, chunk), jnp.bfloat16),
            pltpu.VMEM((n, group, half), jnp.bfloat16),
            pltpu.VMEM((n, group, half), jnp.bfloat16),
            pltpu.VMEM((n, rows, rmax), jnp.float32),
            pltpu.VMEM((n - 1, rows, rmax), jnp.float32),
            dma((7,)), dma((n,)), dma((n,)), dma((n,)), dma((n,)), dma((n,)), dma((n,)), dma((n,)),
        ],
        compiler_params=pltpu.CompilerParams(
            collective_id=0, has_side_effects=True, vmem_limit_bytes=56 * 1024 * 1024
        ),
        cost_estimate=pl.CostEstimate(flops=3 * 10**9, bytes_accessed=4 * 10**7, transcendentals=0),
    )(adapters.T, lengths.T, ranks, tokens, weight, down, up, code)


def fits(mesh, tokens, up):
    n = mesh.shape["dp"]
    chunk, rank_rows = tokens.shape[1] // n, up.shape[1] // n
    return n >= 8 and n & (n - 1) == 0 and n <= 32 and chunk % 128 == 0 and rank_rows % 8 == 0


def solution(mesh):
    in_specs = (
        P(("group", "dp"), None),
        P(),
        P("group", "dp", None),
        P("group", "dp", None),
        P("group"),
        P("group", None),
        P("group", None),
    )
    out_specs = P(("group", "dp"), None)

    def run(*arrays):
        body = fused_local if fits(mesh, arrays[0], arrays[3]) else local
        return jax.shard_map(body, mesh=mesh, in_specs=in_specs, out_specs=out_specs, check_vma=False)(*arrays)

    return run
```

```python
import functools

import jax
import jax.numpy as jnp
import numpy as np
from jax import lax
from jax.experimental import pallas as pl
from jax.experimental.pallas import tpu as pltpu
from jax.sharding import PartitionSpec as P

MESH = pl.DeviceIdType.MESH


RMAX = 128
TOK_DEV = 128
REQ_DEV = 3


adapter_alpha_scale = 32.0


def row_requests(request_length):
    request_ends = jnp.cumsum(request_length, axis=1)
    block_rows = jnp.arange(TOK_DEV, dtype=jnp.int32)
    return jnp.sum(
        (block_rows[None, :, None] >= request_ends[:, None, :]).astype(jnp.int32), axis=2
    )


def finish_rows(base_rows, shrunk, onehot, adapter_ranks, up_panels):
    rank_of_row = jnp.sum(jnp.where(onehot, adapter_ranks[None, :], 0), axis=1)
    within = jnp.arange(RMAX, dtype=jnp.int32)[None, :] < rank_of_row[:, None]
    scaling_factor = adapter_alpha_scale / rank_of_row.astype(jnp.float32)
    scaled = jnp.where(within, shrunk * scaling_factor[:, None], jnp.float32(0.0)).astype(
        jnp.bfloat16
    )
    placed = jnp.where(onehot[:, :, None], scaled[:, None, :], jnp.zeros((), jnp.bfloat16))
    placed = placed.reshape(TOK_DEV, REQ_DEV * RMAX)
    adapter_term = jnp.dot(
        placed, up_panels.reshape(REQ_DEV * RMAX, -1), preferred_element_type=jnp.float32
    )
    return (base_rows + adapter_term).astype(jnp.bfloat16)


def local(
    tokens,
    frozen_projection_weight,
    adapter_down,
    adapter_up,
    adapter_rank,
    request_adapter,
    request_length,
):
    position = lax.axis_index("dp")
    adapter_ids = lax.dynamic_index_in_dim(request_adapter, position, 0, keepdims=False)
    own_lengths = lax.dynamic_index_in_dim(request_length, position, 0, keepdims=False)
    own_ends = jnp.cumsum(own_lengths)
    row_request = jnp.sum(
        (jnp.arange(TOK_DEV, dtype=jnp.int32)[:, None] >= own_ends[None, :]).astype(jnp.int32),
        axis=1,
    )
    onehot = row_request[:, None] == jnp.arange(REQ_DEV, dtype=jnp.int32)[None, :]
    adapter_ranks = jnp.take(adapter_rank, adapter_ids)
    expected_output = request_adapter.T
    columns = lax.all_to_all(tokens, "dp", split_axis=1, concat_axis=0, tiled=True)
    all_requests = row_requests(request_length)
    base_rows = jnp.dot(tokens, frozen_projection_weight, preferred_element_type=jnp.float32)
    block_count = lax.axis_size("dp") * TOK_DEV // TOK_DEV
    row_block = columns
    row_block = row_block.reshape(block_count, TOK_DEV, row_block.shape[1])

    def add_request(request, running):
        panel_rows = jnp.take(adapter_down, jnp.take(request_adapter, request, axis=1), axis=0)
        product = jnp.einsum(
            "ntc,ncr->ntr", row_block, panel_rows, preferred_element_type=jnp.float32
        )
        return running + jnp.where((all_requests == request)[:, :, None], product, jnp.float32(0.0))

    running = lax.fori_loop(
        0, REQ_DEV, add_request, jnp.zeros((block_count, TOK_DEV, RMAX), jnp.float32)
    )
    shrunk = lax.psum_scatter(
        running.reshape(lax.axis_size("dp") * TOK_DEV, RMAX), "dp", scatter_dimension=0, tiled=True
    )
    up_out = jnp.take(adapter_up, expected_output, axis=0)
    up_panels = lax.all_to_all(up_out, "dp", split_axis=1, concat_axis=1, tiled=True)
    up_panels = up_panels.reshape(REQ_DEV, RMAX, -1)
    return finish_rows(base_rows, shrunk, onehot, adapter_ranks, up_panels)


def flip(me, step, n):
    total, weight = 0, 1
    while weight < n:
        total = total + weight * ((me // weight + step // weight) % 2)
        weight *= 2
    return total


AHEAD = 2


def fused(
    n, req,
    adapters_in, lengths_in, ranks_in, tokens, weight, down, up, code,
    out,
    adapters, lengths, ranks, tok, wgt, dwn, upv, codev, base, tok_in, up_out, up_in, part, got,
    load_sem, wgt_sem, tok_send, tok_recv, up_send, up_recv, sum_send, sum_recv,
):
    me = lax.axis_index("dp")
    rows, width = tokens.shape
    chunk = width // n
    far = n // 2
    group, half = up_in.shape[1:]

    loads = [
        pltpu.make_async_copy(source, target, load_sem.at[k])
        for k, (source, target) in enumerate((
            (up, upv), (adapters_in, adapters), (lengths_in, lengths), (ranks_in, ranks),
            (tokens, tok), (down, dwn), (code, codev),
        ))
    ]

    def weight_copy(c):
        piece = pl.ds(pl.multiple_of(c * chunk, chunk), chunk)
        return pltpu.make_async_copy(weight.at[piece], wgt.at[piece], wgt_sem.at[c])

    def token_copy(step):
        peer = flip(me, step, n)
        return pltpu.make_async_remote_copy(
            src_ref=tokens.at[:, pl.ds(pl.multiple_of(peer * chunk, chunk), chunk)],
            dst_ref=tok_in.at[step],
            send_sem=tok_send.at[step], recv_sem=tok_recv.at[step],
            device_id={"dp": peer}, device_id_type=MESH,
        )

    def up_copy(step, arriving=False):
        peer = flip(me, step, n)
        return pltpu.make_async_remote_copy(
            src_ref=up_out.at[peer], dst_ref=up_in.at[peer if arriving else me],
            send_sem=up_send.at[step], recv_sem=up_recv.at[step],
            device_id={"dp": peer}, device_id_type=MESH,
        )

    def sum_copy(level, k):
        slot = n - (n >> level) + k
        return pltpu.make_async_remote_copy(
            src_ref=part.at[(2 * k + 1) << level], dst_ref=got.at[slot],
            send_sem=sum_send.at[slot], recv_sem=sum_recv.at[slot],
            device_id={"dp": flip(me, 1 << level, n)}, device_id_type=MESH,
        )

    barrier = pltpu.get_barrier_semaphore()

    def greet(step, carry):
        pl.semaphore_signal(barrier, inc=1, device_id={"dp": flip(me, step, n)}, device_id_type=MESH)
        return carry

    lax.fori_loop(1, n, greet, 0)
    for load in loads:
        load.start()

    def start_weight(c, carry):
        weight_copy(c).start()
        return carry

    lax.fori_loop(0, n, start_weight, 0)
    pl.semaphore_wait(barrier, n - 1)
    for t in range(AHEAD):
        token_copy(n - 1 - t).start()
        for step in (2 * t, 2 * t + 1):
            if step:
                token_copy(step).start()

    for load in loads[:4]:
        load.wait()

    def pick_up(i, carry):
        panels = [upv[adapters[q, i]].astype(jnp.float32) for q in range(req)]
        picked = [p[:, h * half:(h + 1) * half] for h in range(2) for p in panels]
        up_out[i] = jnp.concatenate(picked, axis=0).astype(jnp.bfloat16)
        return carry

    lax.fori_loop(0, n, pick_up, 0)
    up_in[me] = up_out[me]

    row = lax.broadcasted_iota(jnp.int32, (rows, 1), 0)

    def shrink(step):
        i = flip(me, step, n)
        block = tok_in[step]
        total = jnp.dot(block, dwn[adapters[0, i]], preferred_element_type=jnp.float32)
        end = jnp.int32(0)
        for q in range(1, req):
            end = end + lengths[q - 1, i]
            product = jnp.dot(block, dwn[adapters[q, i]], preferred_element_type=jnp.float32)
            total = jnp.where(row >= end, product, total)
        part[step] = total

    def add_base(c, carry):
        weight_copy(c).wait()
        piece = pl.ds(pl.multiple_of(c * chunk, chunk), chunk)
        base[...] += jnp.dot(tok[:, piece], wgt[piece, :], preferred_element_type=jnp.float32)
        return carry

    ready, moving, sent = set(), [], []

    def mark(level, block):
        ready.add((level, block))
        k = block // 2
        if block % 2:
            sum_copy(level, k).start()
            sent.append((level, k))
        if {(level, 2 * k), (level, 2 * k + 1)} <= ready:
            moving.append((level, k))

    def absorb():
        level, k = moving.pop(0)
        sum_copy(level, k).wait_recv()
        kept = (2 * k) << level
        part[kept] = part[kept] + got[n - (n >> level) + k]
        mark(level + 1, k)

    ups = list(range(far, n))

    def start_ups(count):
        for step in ups[:count]:
            up_copy(step).start()
        del ups[:count]

    for t in range(far):
        near = [step for step in (2 * t, 2 * t + 1) if step < far]
        for _ in range(len(moving)):
            absorb()
        if t == 0:
            for load in loads[4:]:
                load.wait()
            tok_in[0] = tok[:, pl.ds(pl.multiple_of(me * chunk, chunk), chunk)]
            base[...] = jnp.zeros_like(base)
        for step in near:
            if step:
                token_copy(step).wait_recv()
            if step + 2 * AHEAD < far:
                token_copy(step + 2 * AHEAD).start()
        if t:
            up_copy(t).start()
        lax.fori_loop(2 * t, 2 * t + 2, add_base, 0)
        if near:
            def one(step, carry):
                shrink(step)
                return carry

            lax.fori_loop(near[0], near[-1] + 1, one, 0)
            for step in near:
                mark(0, step)
        last = n - 1 - t
        token_copy(last).wait_recv()
        if t + AHEAD < far:
            token_copy(last - AHEAD).start()
        else:
            start_ups(2)
        shrink(last)
        mark(0, last)
    while moving:
        if moving[0][0] == n.bit_length() - 2:
            start_ups(n)
        absorb()
    shrunk = part[0]

    request = jnp.zeros((rows, 1), jnp.int32)
    rank = jnp.zeros((rows, 1), jnp.int32) + ranks[adapters[0, me]]
    end = jnp.int32(0)
    for q in range(1, req):
        end = end + lengths[q - 1, me]
        later = row >= end
        request = jnp.where(later, q, request)
        rank = jnp.where(later, ranks[adapters[q, me]], rank)
    within = lax.broadcasted_iota(jnp.int32, shrunk.shape, 1) < rank
    factor = 32.0 / rank.astype(jnp.float32)
    scaled = jnp.where(within, shrunk * factor, 0.0).astype(jnp.bfloat16)
    span = far * group
    codes = codev[0:1, 0:span]
    rank_index = lax.broadcasted_iota(jnp.int32, (shrunk.shape[1], span), 0)

    def await_up(step, carry):
        up_copy(step, arriving=True).wait_recv()
        return carry

    near_side = me // far
    for side, steps in ((near_side, (1, far)), (1 - near_side, (far, n))):
        rank_of = codev[1:2, pl.ds(pl.multiple_of(side * span, span), span)]
        picked = jnp.where(rank_index == rank_of, 1.0, 0.0).astype(jnp.bfloat16)
        spread_out = jnp.dot(scaled, picked, preferred_element_type=jnp.float32)
        placed = [
            jnp.where(codes == request + h * req, spread_out, 0.0).astype(jnp.bfloat16) for h in range(2)
        ]
        lax.fori_loop(*steps, await_up, 0)
        panels = up_in[pl.ds(side * far, far)].reshape(span, half)
        for h in range(2):
            piece = slice(h * half, (h + 1) * half)
            total = base[:, piece] + jnp.dot(placed[h], panels, preferred_element_type=jnp.float32)
            if steps[0] == 1:
                base[:, piece] = total
            else:
                out[:, piece] = total.astype(jnp.bfloat16)

    def await_sent(step, carry):
        token_copy(step).wait_send()
        up_copy(step).wait_send()
        return carry

    lax.fori_loop(1, n, await_sent, 0)
    for pair in sent:
        sum_copy(*pair).wait_send()


def fused_local(tokens, weight, down, up, ranks, adapters, lengths):
    n = lax.axis_size("dp")
    rows, width = tokens.shape
    chunk = width // n
    columns = weight.shape[1]
    req = adapters.shape[1]
    rank_rows, rmax = up.shape[1], down.shape[2]
    half = columns // 2
    group = 2 * req * rank_rows
    spread = n * group
    slot = np.arange(spread)
    rank_of = (slot // group) * rank_rows + slot % rank_rows
    code = np.zeros((8, spread), np.int32)
    code[0], code[1] = (slot % group) // rank_rows, rank_of
    code = jnp.asarray(code)
    dma = pltpu.SemaphoreType.DMA
    return pl.pallas_call(
        functools.partial(fused, n, req),
        out_shape=jax.ShapeDtypeStruct((rows, columns), jnp.bfloat16),
        in_specs=[pl.BlockSpec(memory_space=pl.ANY)] * 8,
        out_specs=pl.BlockSpec(memory_space=pltpu.VMEM),
        scratch_shapes=[
            pltpu.SMEM(adapters.shape[::-1], jnp.int32),
            pltpu.SMEM(lengths.shape[::-1], jnp.int32),
            pltpu.SMEM(ranks.shape, jnp.int32),
            pltpu.VMEM((rows, width), jnp.bfloat16),
            pltpu.VMEM(weight.shape, jnp.bfloat16),
            pltpu.VMEM(down.shape, jnp.bfloat16),
            pltpu.VMEM(up.shape, jnp.bfloat16),
            pltpu.VMEM(code.shape, jnp.int32),
            pltpu.VMEM((rows, columns), jnp.float32),
            pltpu.VMEM((n, rows, chunk), jnp.bfloat16),
            pltpu.VMEM((n, group, half), jnp.bfloat16),
            pltpu.VMEM((n, group, half), jnp.bfloat16),
            pltpu.VMEM((n, rows, rmax), jnp.float32),
            pltpu.VMEM((n - 1, rows, rmax), jnp.float32),
            dma((7,)), dma((n,)), dma((n,)), dma((n,)), dma((n,)), dma((n,)), dma((n,)), dma((n,)),
        ],
        compiler_params=pltpu.CompilerParams(
            collective_id=0, has_side_effects=True, vmem_limit_bytes=56 * 1024 * 1024
        ),
        cost_estimate=pl.CostEstimate(flops=3 * 10**9, bytes_accessed=4 * 10**7, transcendentals=0),
    )(adapters.T, lengths.T, ranks, tokens, weight, down, up, code)


def fits(mesh, tokens, up):
    n = mesh.shape["dp"]
    chunk, rank_rows = tokens.shape[1] // n, up.shape[1] // n
    return n >= 8 and n & (n - 1) == 0 and n <= 32 and chunk % 128 == 0 and rank_rows % 8 == 0


def solution(mesh):
    in_specs = (
        P(("group", "dp"), None),
        P(),
        P("group", "dp", None),
        P("group", "dp", None),
        P("group"),
        P("group", None),
        P("group", None),
    )
    out_specs = P(("group", "dp"), None)

    def run(*arrays):
        body = fused_local if fits(mesh, arrays[0], arrays[3]) else local
        return jax.shard_map(body, mesh=mesh, in_specs=in_specs, out_specs=out_specs, check_vma=False)(*arrays)

    return run
```

```python
import functools

import jax
import jax.numpy as jnp
import numpy as np
from jax import lax
from jax.experimental import pallas as pl
from jax.experimental.pallas import tpu as pltpu
from jax.sharding import PartitionSpec as P

MESH = pl.DeviceIdType.MESH


RMAX = 128
TOK_DEV = 128
REQ_DEV = 3


adapter_alpha_scale = 32.0


def row_requests(request_length):
    request_ends = jnp.cumsum(request_length, axis=1)
    block_rows = jnp.arange(TOK_DEV, dtype=jnp.int32)
    return jnp.sum(
        (block_rows[None, :, None] >= request_ends[:, None, :]).astype(jnp.int32), axis=2
    )


def finish_rows(base_rows, shrunk, onehot, adapter_ranks, up_panels):
    rank_of_row = jnp.sum(jnp.where(onehot, adapter_ranks[None, :], 0), axis=1)
    within = jnp.arange(RMAX, dtype=jnp.int32)[None, :] < rank_of_row[:, None]
    scaling_factor = adapter_alpha_scale / rank_of_row.astype(jnp.float32)
    scaled = jnp.where(within, shrunk * scaling_factor[:, None], jnp.float32(0.0)).astype(
        jnp.bfloat16
    )
    placed = jnp.where(onehot[:, :, None], scaled[:, None, :], jnp.zeros((), jnp.bfloat16))
    placed = placed.reshape(TOK_DEV, REQ_DEV * RMAX)
    adapter_term = jnp.dot(
        placed, up_panels.reshape(REQ_DEV * RMAX, -1), preferred_element_type=jnp.float32
    )
    return (base_rows + adapter_term).astype(jnp.bfloat16)


def local(
    tokens,
    frozen_projection_weight,
    adapter_down,
    adapter_up,
    adapter_rank,
    request_adapter,
    request_length,
):
    position = lax.axis_index("dp")
    adapter_ids = lax.dynamic_index_in_dim(request_adapter, position, 0, keepdims=False)
    own_lengths = lax.dynamic_index_in_dim(request_length, position, 0, keepdims=False)
    own_ends = jnp.cumsum(own_lengths)
    row_request = jnp.sum(
        (jnp.arange(TOK_DEV, dtype=jnp.int32)[:, None] >= own_ends[None, :]).astype(jnp.int32),
        axis=1,
    )
    onehot = row_request[:, None] == jnp.arange(REQ_DEV, dtype=jnp.int32)[None, :]
    adapter_ranks = jnp.take(adapter_rank, adapter_ids)
    expected_output = request_adapter.T
    columns = lax.all_to_all(tokens, "dp", split_axis=1, concat_axis=0, tiled=True)
    all_requests = row_requests(request_length)
    base_rows = jnp.dot(tokens, frozen_projection_weight, preferred_element_type=jnp.float32)
    block_count = lax.axis_size("dp") * TOK_DEV // TOK_DEV
    row_block = columns
    row_block = row_block.reshape(block_count, TOK_DEV, row_block.shape[1])

    def add_request(request, running):
        panel_rows = jnp.take(adapter_down, jnp.take(request_adapter, request, axis=1), axis=0)
        product = jnp.einsum(
            "ntc,ncr->ntr", row_block, panel_rows, preferred_element_type=jnp.float32
        )
        return running + jnp.where((all_requests == request)[:, :, None], product, jnp.float32(0.0))

    running = lax.fori_loop(
        0, REQ_DEV, add_request, jnp.zeros((block_count, TOK_DEV, RMAX), jnp.float32)
    )
    shrunk = lax.psum_scatter(
        running.reshape(lax.axis_size("dp") * TOK_DEV, RMAX), "dp", scatter_dimension=0, tiled=True
    )
    up_out = jnp.take(adapter_up, expected_output, axis=0)
    up_panels = lax.all_to_all(up_out, "dp", split_axis=1, concat_axis=1, tiled=True)
    up_panels = up_panels.reshape(REQ_DEV, RMAX, -1)
    return finish_rows(base_rows, shrunk, onehot, adapter_ranks, up_panels)


def flip(me, step, n):
    total, weight = 0, 1
    while weight < n:
        total = total + weight * ((me // weight + step // weight) % 2)
        weight *= 2
    return total


AHEAD = 3


def fused(
    n, req,
    adapters_in, lengths_in, ranks_in, tokens, weight, down, up, code,
    out,
    adapters, lengths, ranks, tok, wgt, dwn, upv, codev, base, tok_in, up_out, up_in, part, got,
    load_sem, wgt_sem, tok_send, tok_recv, up_send, up_recv, sum_send, sum_recv,
):
    me = lax.axis_index("dp")
    rows, width = tokens.shape
    chunk = width // n
    far = n // 2
    group, half = up_in.shape[1:]

    loads = [
        pltpu.make_async_copy(source, target, load_sem.at[k])
        for k, (source, target) in enumerate((
            (up, upv), (adapters_in, adapters), (lengths_in, lengths), (ranks_in, ranks),
            (tokens, tok), (down, dwn), (code, codev),
        ))
    ]

    def weight_copy(c):
        piece = pl.ds(pl.multiple_of(c * chunk, chunk), chunk)
        return pltpu.make_async_copy(weight.at[piece], wgt.at[piece], wgt_sem.at[c])

    def token_copy(step):
        peer = flip(me, step, n)
        return pltpu.make_async_remote_copy(
            src_ref=tokens.at[:, pl.ds(pl.multiple_of(peer * chunk, chunk), chunk)],
            dst_ref=tok_in.at[step],
            send_sem=tok_send.at[step], recv_sem=tok_recv.at[step],
            device_id={"dp": peer}, device_id_type=MESH,
        )

    def up_copy(step, arriving=False):
        peer = flip(me, step, n)
        return pltpu.make_async_remote_copy(
            src_ref=up_out.at[peer], dst_ref=up_in.at[peer if arriving else me],
            send_sem=up_send.at[step], recv_sem=up_recv.at[step],
            device_id={"dp": peer}, device_id_type=MESH,
        )

    def sum_copy(level, k):
        slot = n - (n >> level) + k
        return pltpu.make_async_remote_copy(
            src_ref=part.at[(2 * k + 1) << level], dst_ref=got.at[slot],
            send_sem=sum_send.at[slot], recv_sem=sum_recv.at[slot],
            device_id={"dp": flip(me, 1 << level, n)}, device_id_type=MESH,
        )

    barrier = pltpu.get_barrier_semaphore()

    def greet(step, carry):
        pl.semaphore_signal(barrier, inc=1, device_id={"dp": flip(me, step, n)}, device_id_type=MESH)
        return carry

    lax.fori_loop(1, n, greet, 0)
    for load in loads:
        load.start()

    def start_weight(c, carry):
        weight_copy(c).start()
        return carry

    lax.fori_loop(0, n, start_weight, 0)
    pl.semaphore_wait(barrier, n - 1)
    for t in range(AHEAD):
        token_copy(n - 1 - t).start()
        for step in (2 * t, 2 * t + 1):
            if step:
                token_copy(step).start()

    for load in loads[:4]:
        load.wait()

    def pick_up(i, carry):
        panels = [upv[adapters[q, i]].astype(jnp.float32) for q in range(req)]
        picked = [p[:, h * half:(h + 1) * half] for h in range(2) for p in panels]
        up_out[i] = jnp.concatenate(picked, axis=0).astype(jnp.bfloat16)
        return carry

    lax.fori_loop(0, n, pick_up, 0)
    up_in[me] = up_out[me]

    row = lax.broadcasted_iota(jnp.int32, (rows, 1), 0)

    def shrink(step):
        i = flip(me, step, n)
        block = tok_in[step]
        total = jnp.dot(block, dwn[adapters[0, i]], preferred_element_type=jnp.float32)
        end = jnp.int32(0)
        for q in range(1, req):
            end = end + lengths[q - 1, i]
            product = jnp.dot(block, dwn[adapters[q, i]], preferred_element_type=jnp.float32)
            total = jnp.where(row >= end, product, total)
        part[step] = total

    def add_base(c, carry):
        weight_copy(c).wait()
        piece = pl.ds(pl.multiple_of(c * chunk, chunk), chunk)
        base[...] += jnp.dot(tok[:, piece], wgt[piece, :], preferred_element_type=jnp.float32)
        return carry

    ready, moving, sent = set(), [], []

    def mark(level, block):
        ready.add((level, block))
        k = block // 2
        if block % 2:
            sum_copy(level, k).start()
            sent.append((level, k))
        if {(level, 2 * k), (level, 2 * k + 1)} <= ready:
            moving.append((level, k))

    def absorb():
        level, k = moving.pop(0)
        sum_copy(level, k).wait_recv()
        kept = (2 * k) << level
        part[kept] = part[kept] + got[n - (n >> level) + k]
        mark(level + 1, k)

    ups = list(range(far, n))

    def start_ups(count):
        for step in ups[:count]:
            up_copy(step).start()
        del ups[:count]

    for t in range(far):
        near = [step for step in (2 * t, 2 * t + 1) if step < far]
        for _ in range(len(moving)):
            absorb()
        if t == 0:
            for load in loads[4:]:
                load.wait()
            tok_in[0] = tok[:, pl.ds(pl.multiple_of(me * chunk, chunk), chunk)]
            base[...] = jnp.zeros_like(base)
        for step in near:
            if step:
                token_copy(step).wait_recv()
            if step + 2 * AHEAD < far:
                token_copy(step + 2 * AHEAD).start()
        if t:
            up_copy(t).start()
        lax.fori_loop(2 * t, 2 * t + 2, add_base, 0)
        if near:
            def one(step, carry):
                shrink(step)
                return carry

            lax.fori_loop(near[0], near[-1] + 1, one, 0)
            for step in near:
                mark(0, step)
        last = n - 1 - t
        token_copy(last).wait_recv()
        if t + AHEAD < far:
            token_copy(last - AHEAD).start()
        else:
            start_ups(1 if t + AHEAD == far else 2)
        shrink(last)
        mark(0, last)
    while moving:
        if moving[0][0] == n.bit_length() - 2:
            start_ups(n)
        absorb()
    shrunk = part[0]

    request = jnp.zeros((rows, 1), jnp.int32)
    rank = jnp.zeros((rows, 1), jnp.int32) + ranks[adapters[0, me]]
    end = jnp.int32(0)
    for q in range(1, req):
        end = end + lengths[q - 1, me]
        later = row >= end
        request = jnp.where(later, q, request)
        rank = jnp.where(later, ranks[adapters[q, me]], rank)
    within = lax.broadcasted_iota(jnp.int32, shrunk.shape, 1) < rank
    factor = 32.0 / rank.astype(jnp.float32)
    scaled = jnp.where(within, shrunk * factor, 0.0).astype(jnp.bfloat16)
    span = far * group
    codes = codev[0:1, 0:span]
    rank_index = lax.broadcasted_iota(jnp.int32, (shrunk.shape[1], span), 0)

    def await_up(step, carry):
        up_copy(step, arriving=True).wait_recv()
        return carry

    near_side = me // far
    for side, steps in ((near_side, (1, far)), (1 - near_side, (far, n))):
        rank_of = codev[1:2, pl.ds(pl.multiple_of(side * span, span), span)]
        picked = jnp.where(rank_index == rank_of, 1.0, 0.0).astype(jnp.bfloat16)
        spread_out = jnp.dot(scaled, picked, preferred_element_type=jnp.float32)
        placed = [
            jnp.where(codes == request + h * req, spread_out, 0.0).astype(jnp.bfloat16) for h in range(2)
        ]
        lax.fori_loop(*steps, await_up, 0)
        panels = up_in[pl.ds(side * far, far)].reshape(span, half)
        for h in range(2):
            piece = slice(h * half, (h + 1) * half)
            total = base[:, piece] + jnp.dot(placed[h], panels, preferred_element_type=jnp.float32)
            if steps[0] == 1:
                base[:, piece] = total
            else:
                out[:, piece] = total.astype(jnp.bfloat16)

    def await_sent(step, carry):
        token_copy(step).wait_send()
        up_copy(step).wait_send()
        return carry

    lax.fori_loop(1, n, await_sent, 0)
    for pair in sent:
        sum_copy(*pair).wait_send()


def fused_local(tokens, weight, down, up, ranks, adapters, lengths):
    n = lax.axis_size("dp")
    rows, width = tokens.shape
    chunk = width // n
    columns = weight.shape[1]
    req = adapters.shape[1]
    rank_rows, rmax = up.shape[1], down.shape[2]
    half = columns // 2
    group = 2 * req * rank_rows
    spread = n * group
    slot = np.arange(spread)
    rank_of = (slot // group) * rank_rows + slot % rank_rows
    code = np.zeros((8, spread), np.int32)
    code[0], code[1] = (slot % group) // rank_rows, rank_of
    code = jnp.asarray(code)
    dma = pltpu.SemaphoreType.DMA
    return pl.pallas_call(
        functools.partial(fused, n, req),
        out_shape=jax.ShapeDtypeStruct((rows, columns), jnp.bfloat16),
        in_specs=[pl.BlockSpec(memory_space=pl.ANY)] * 8,
        out_specs=pl.BlockSpec(memory_space=pltpu.VMEM),
        scratch_shapes=[
            pltpu.SMEM(adapters.shape[::-1], jnp.int32),
            pltpu.SMEM(lengths.shape[::-1], jnp.int32),
            pltpu.SMEM(ranks.shape, jnp.int32),
            pltpu.VMEM((rows, width), jnp.bfloat16),
            pltpu.VMEM(weight.shape, jnp.bfloat16),
            pltpu.VMEM(down.shape, jnp.bfloat16),
            pltpu.VMEM(up.shape, jnp.bfloat16),
            pltpu.VMEM(code.shape, jnp.int32),
            pltpu.VMEM((rows, columns), jnp.float32),
            pltpu.VMEM((n, rows, chunk), jnp.bfloat16),
            pltpu.VMEM((n, group, half), jnp.bfloat16),
            pltpu.VMEM((n, group, half), jnp.bfloat16),
            pltpu.VMEM((n, rows, rmax), jnp.float32),
            pltpu.VMEM((n - 1, rows, rmax), jnp.float32),
            dma((7,)), dma((n,)), dma((n,)), dma((n,)), dma((n,)), dma((n,)), dma((n,)), dma((n,)),
        ],
        compiler_params=pltpu.CompilerParams(
            collective_id=0, has_side_effects=True, vmem_limit_bytes=56 * 1024 * 1024
        ),
        cost_estimate=pl.CostEstimate(flops=3 * 10**9, bytes_accessed=4 * 10**7, transcendentals=0),
    )(adapters.T, lengths.T, ranks, tokens, weight, down, up, code)


def fits(mesh, tokens, up):
    n = mesh.shape["dp"]
    chunk, rank_rows = tokens.shape[1] // n, up.shape[1] // n
    return n >= 8 and n & (n - 1) == 0 and n <= 32 and chunk % 128 == 0 and rank_rows % 8 == 0


def solution(mesh):
    in_specs = (
        P(("group", "dp"), None),
        P(),
        P("group", "dp", None),
        P("group", "dp", None),
        P("group"),
        P("group", None),
        P("group", None),
    )
    out_specs = P(("group", "dp"), None)

    def run(*arrays):
        body = fused_local if fits(mesh, arrays[0], arrays[3]) else local
        return jax.shard_map(body, mesh=mesh, in_specs=in_specs, out_specs=out_specs, check_vma=False)(*arrays)

    return run
```
